32 devices in a mesh: row: 4 (over y, x), col: 8 (over z, core).
Axes of the slice: x: 2, y: 2, z: 4, core: 2. Of those that a mesh axis runs over, the one named last changes fastest.
Arguments:
- frames: bfloat16 [256, 8192], P('col', 'row'), may hold values from -6 to 6
- cotangent: bfloat16 [256, 8192], P('col', 'row'), may hold values from -6 to 6
- gate_weight: bfloat16 [8192, 14336], P('row', 'col'), may hold values from -0.0625 to 0.0625
- up_weight: bfloat16 [8192, 14336], P('row', 'col'), may hold values from -0.0625 to 0.0625
- down_weight: bfloat16 [14336, 8192], P('col', 'row'), may hold values from -0.046875 to 0.046875
- utt_ids: int32 [256], replicated, may hold values from 0 to 15, never falling along the last dimension, each value on 1 to 32 neighbouring positions
- valid_len: int32 [16], replicated, may hold values from 1 to 32
- time_start: int32 [16], replicated, may hold values from 0 to 31
- time_width: int32 [16], replicated, may hold values from 0 to 8
- freq_start: int32 [16], replicated, may hold values from 0 to 8191
- freq_width: int32 [16], replicated, may hold values from 0 to 2048
Outputs:
- output: bfloat16 [256, 8192], P('col', 'row')
- grad_frames: bfloat16 [256, 8192], P('col', 'row')
- grad_gate: bfloat16 [8192, 14336], P('row', 'col')
- grad_up: bfloat16 [8192, 14336], P('row', 'col')
- grad_down: bfloat16 [14336, 8192], P('col', 'row')
The draws below stay inside these ranges and needn't reach their ends.
Inputs may be any that keep to these rules, and one draw needn't show every extreme that they name: `utt_ids`: token ids never fall along the tokens; each utterance holds 1 to 32 tokens.
All inputs are finite; a program needn't handle non-finite values.
Results may differ from the reference program's by a relative error of at most 0.025.
Values may be sent and summed in bfloat16 or wider, within the bound.
A program may use at most 128 MiB of HBM per device.

```python
import math
import jax
import jax.numpy as jnp
import numpy as np
from jax import lax

D = 8192
FF = 14336
UTTS = 16
TOKENS = 256
MOSTLEN = 32
TIME_SPAN = 8
FREQ_SPAN = 2048
N_ROW = 4
N_COL = 8


def set_ends(values, key, least, largest):
    spot = [jax.random.randint(jax.random.fold_in(key, axis), (), 0, length) for axis, length in enumerate(values.shape)]
    main_axis = values.shape.index(max(values.shape))
    next_to = spot[:main_axis] + [(spot[main_axis] + 1) % values.shape[main_axis]] + spot[main_axis + 1:]
    return values.at[tuple(spot)].set(least).at[tuple(next_to)].set(largest)


def block_scale(own_key, extent, shards, smallest, top_value):
    factor_of = 1.0
    for axis_at, blocks in shards:
        heights = jax.random.uniform(jax.random.fold_in(jax.random.fold_in(own_key, 6), axis_at), (blocks,), jnp.float32, smallest / len(shards), top_value / len(shards))
        factor_of = factor_of * jnp.repeat(jnp.exp(heights), extent[axis_at] // blocks).reshape((-1,) + (1,) * (len(extent) - 1 - axis_at))
    return factor_of


def profile(number_of, total, limit, skew):
    weights = [(1 << 20) // math.isqrt(grade ** skew) + 1 for grade in range(2, number_of + 1)]
    spare, holding = total - limit - (number_of - 1), [1] * (number_of - 1)
    while spare > 0:
        candidates = [i for i in range(number_of - 1) if holding[i] < limit]
        whole, budget = sum([weights[i] for i in candidates]), spare
        for i in candidates:
            extra = min(limit - holding[i], max(1, budget * weights[i] // whole), spare)
            holding[i] = holding[i] + extra
            spare = spare - extra
    return np.array([limit] + holding)


def ragged(rng, number_of, total, limit, slope):
    if number_of == 2:
        one = jax.random.randint(rng, (), max(1, total - limit), min(limit, total - 1) + 1)
        return jnp.stack([one, total - one])
    lengths = jnp.asarray(profile(number_of, total, limit, slope), jnp.int32)
    couples = (number_of - 1) // 2
    donor, taker = lengths[1:1 + 2 * couples:2], lengths[2:2 + 2 * couples:2]
    room = jnp.minimum(donor - 1, limit - taker)
    moved = jax.random.randint(jax.random.fold_in(rng, 1), (couples,), 0, 1 << 20) % (room + 1)
    lengths = lengths.at[1:1 + 2 * couples:2].set(donor - moved).at[2:2 + 2 * couples:2].set(taker + moved)
    return lengths[jax.random.permutation(jax.random.fold_in(rng, 2), number_of)]


def scatter_about(own_key, dims, scale, most, cuts=(), kind=jnp.bfloat16):
    level = block_scale(own_key, dims, cuts, -0.22, 0.18) if cuts else 1.0
    entries = jax.random.normal(own_key, dims, jnp.float32) * scale * level
    return jnp.minimum(jnp.maximum(entries, -most), most).astype(kind)


def setup_inputs(seed: int = 0) -> dict:
    key_list = jax.random.split(jax.random.key(seed), 12)
    return {
        "frames": scatter_about(key_list[0], (TOKENS, D), 1.0, 6.0, ((0, 8), (1, 4))),
        "cotangent": scatter_about(key_list[1], (TOKENS, D), 1.0, 6.0, ((0, 8), (1, 4))),
        "gate_weight": scatter_about(key_list[2], (D, FF), D ** -0.5, 0.0625, ((0, 4), (1, 8))),
        "up_weight": scatter_about(key_list[3], (D, FF), D ** -0.5, 0.0625, ((0, 4), (1, 8))),
        "down_weight": scatter_about(key_list[4], (FF, D), FF ** -0.5, 0.046875, ((0, 8), (1, 4))),
        "utt_ids": jnp.searchsorted(jnp.cumsum(ragged(key_list[5], UTTS, TOKENS, MOSTLEN, 0)), jnp.arange(TOKENS), side="right").astype(jnp.int32),
        "valid_len": set_ends(jax.random.randint(key_list[6], (UTTS,), 1, MOSTLEN + 1), jax.random.fold_in(key_list[6], 1), 1, MOSTLEN).astype(jnp.int32),
        "time_start": set_ends(jax.random.randint(key_list[7], (UTTS,), 0, MOSTLEN), jax.random.fold_in(key_list[7], 1), 0, MOSTLEN - 1).astype(jnp.int32),
        "time_width": set_ends(jax.random.randint(key_list[8], (UTTS,), 0, TIME_SPAN + 1), jax.random.fold_in(key_list[8], 1), 0, TIME_SPAN).astype(jnp.int32),
        "freq_start": set_ends(jax.random.randint(key_list[9], (UTTS,), 0, D), jax.random.fold_in(key_list[9], 1), 0, D - 1).astype(jnp.int32),
        "freq_width": set_ends(jax.random.randint(key_list[10], (UTTS,), 0, FREQ_SPAN + 1), jax.random.fold_in(key_list[10], 1), 0, FREQ_SPAN).astype(jnp.int32),
    }


def span_masks(utt_ids, local_ids, tok_index, feat_index, valid_len, time_start, time_width, freq_start, freq_width):
    utt_index = jnp.arange(valid_len.shape[0], dtype=jnp.int32)
    starts = jnp.sum((utt_ids[None, :] < utt_index[:, None]).astype(jnp.int32), axis=1)
    member = (local_ids[:, None] == utt_index[None, :]).astype(jnp.int32)

    def lookup(table):
        return jnp.sum(member * table[None, :], axis=1)

    position = tok_index - lookup(starts)
    valid_rows = position < lookup(valid_len)
    time_low = lookup(time_start)
    in_time = (position >= time_low) & (position < time_low + lookup(time_width))
    freq_low = lookup(freq_start)[:, None]
    freq_high = freq_low + lookup(freq_width)[:, None]
    in_freq = (feat_index[None, :] >= freq_low) & (feat_index[None, :] < freq_high)
    keep_mask = (valid_rows & jnp.logical_not(in_time))[:, None] & jnp.logical_not(in_freq)
    return keep_mask, valid_rows


def rounded(value):
    return lax.optimization_barrier(value.astype(jnp.bfloat16)).astype(jnp.float32)


def blockwise(term, blocks, rows, cols):
    def step(index, total):
        return total + rounded(term(index))

    return lax.fori_loop(0, blocks, step, jnp.zeros((rows, cols), jnp.float32))


def reference(frames, cotangent, gate_weight, up_weight, down_weight, utt_ids, valid_len, time_start, time_width, freq_start, freq_width):
    total = frames.shape[0]
    width = frames.shape[1]
    hidden_units = gate_weight.shape[1]
    feat_block = width // N_ROW
    unit_block = hidden_units // N_COL
    tok_index = jnp.arange(total, dtype=jnp.int32)
    feat_index = jnp.arange(width, dtype=jnp.int32)
    keep_mask, valid_rows = span_masks(utt_ids, utt_ids, tok_index, feat_index, valid_len, time_start, time_width, freq_start, freq_width)
    masked = jnp.where(keep_mask, frames, jnp.zeros_like(frames))
    contract_last = (((1,), (1,)), ((), ()))
    contract_first = (((0,), (0,)), ((), ()))

    def feat_slice(array, index, axis):
        return lax.dynamic_slice_in_dim(array, (index * feat_block).astype(jnp.int32), feat_block, axis)

    def unit_slice(array, index, axis):
        return lax.dynamic_slice_in_dim(array, (index * unit_block).astype(jnp.int32), unit_block, axis)

    def gate_term(index):
        return jnp.dot(feat_slice(masked, index, 1), feat_slice(gate_weight, index, 0), preferred_element_type=jnp.float32)

    def up_term(index):
        return jnp.dot(feat_slice(masked, index, 1), feat_slice(up_weight, index, 0), preferred_element_type=jnp.float32)

    gate = blockwise(gate_term, N_ROW, total, hidden_units)
    up = blockwise(up_term, N_ROW, total, hidden_units)
    sigmoid_gate = jax.nn.sigmoid(gate)
    hidden = (gate * sigmoid_gate * up).astype(jnp.bfloat16)

    def output_term(index):
        return jnp.dot(unit_slice(hidden, index, 1), unit_slice(down_weight, index, 0), preferred_element_type=jnp.float32)

    output = blockwise(output_term, N_COL, total, width).astype(jnp.bfloat16)
    cot_valid = jnp.where(valid_rows[:, None], cotangent, jnp.zeros_like(cotangent))

    def hidden_grad_term(index):
        return lax.dot_general(feat_slice(cot_valid, index, 1), feat_slice(down_weight, index, 1), contract_last, preferred_element_type=jnp.float32)

    grad_hidden = blockwise(hidden_grad_term, N_ROW, total, hidden_units)
    dgate = (grad_hidden * up * sigmoid_gate * (1.0 + gate * (1.0 - sigmoid_gate))).astype(jnp.bfloat16)
    dup = (grad_hidden * gate * sigmoid_gate).astype(jnp.bfloat16)
    grad_down = lax.dot_general(hidden, cot_valid, contract_first, preferred_element_type=jnp.float32).astype(jnp.bfloat16)
    grad_gate = lax.dot_general(masked, dgate, contract_first, preferred_element_type=jnp.float32).astype(jnp.bfloat16)
    grad_up = lax.dot_general(masked, dup, contract_first, preferred_element_type=jnp.float32).astype(jnp.bfloat16)

    def input_grad_term(index):
        first = lax.dot_general(unit_slice(dgate, index, 1), unit_slice(gate_weight, index, 1), contract_last, preferred_element_type=jnp.float32)
        second = lax.dot_general(unit_slice(dup, index, 1), unit_slice(up_weight, index, 1), contract_last, preferred_element_type=jnp.float32)
        return first + second

    grad_masked = blockwise(input_grad_term, N_COL, total, width)
    grad_frames = jnp.where(keep_mask, grad_masked, jnp.zeros_like(grad_masked)).astype(jnp.bfloat16)
    return (output, grad_frames, grad_gate, grad_up, grad_down)
```

```python
import functools
import jax
import jax.numpy as jnp
from jax import lax
from jax.experimental import pallas as pl
from jax.experimental.pallas import tpu as pltpu
from jax.sharding import PartitionSpec as P


def span_masks(
    utt_ids,
    local_ids,
    tok_index,
    feat_index,
    valid_len,
    time_start,
    time_width,
    freq_start,
    freq_width,
):
    utt_index = jnp.arange(valid_len.shape[0], dtype=jnp.int32)
    starts = jnp.sum((utt_ids[None, :] < utt_index[:, None]).astype(jnp.int32), axis=1)
    member = (local_ids[:, None] == utt_index[None, :]).astype(jnp.int32)

    def lookup(table):
        return jnp.sum(member * table[None, :], axis=1)

    position = tok_index - lookup(starts)
    valid_rows = position < lookup(valid_len)
    time_low = lookup(time_start)
    in_time = (position >= time_low) & (position < time_low + lookup(time_width))
    freq_low = lookup(freq_start)[:, None]
    freq_high = freq_low + lookup(freq_width)[:, None]
    in_freq = (feat_index[None, :] >= freq_low) & (feat_index[None, :] < freq_high)
    keep_mask = (valid_rows & jnp.logical_not(in_time))[:, None] & jnp.logical_not(in_freq)
    return (keep_mask, valid_rows)


MESH_ID = pl.DeviceIdType.MESH
LAST = (((1,), (1,)), ((), ()))
FIRST = (((0,), (0,)), ((), ()))
F32 = jnp.float32
BF16 = jnp.bfloat16


def dot(a, b):
    return jnp.dot(a, b, preferred_element_type=F32)


def dot_last(a, b):
    return lax.dot_general(a, b, LAST, preferred_element_type=F32)


def exchange_kernel(
    R,
    C,
    masked,
    cot,
    gate_hbm,
    up_hbm,
    down_hbm,
    out,
    gmask,
    tok_hbm,
    cotall_hbm,
    hid_hbm,
    dg_hbm,
    du_hbm,
    gw,
    uw,
    dw,
    rows,
    gu_send,
    gu_recv,
    gh_send,
    gh_recv,
    gate_s,
    up_s,
    act,
    part,
    sib_recv,
    z_send,
    z_recv,
    w_sem,
    o_sem,
    ag_s,
    ag_r,
    fw_s,
    fw_r,
    gu_ss,
    gu_rs,
    gh_ss,
    gh_rs,
    act_ss,
    act_rs,
    sib_ss,
    sib_rs,
    z_ss,
    z_rs,
):
    r = lax.axis_index("row")
    c = lax.axis_index("col")
    z = c // 2
    k = c % 2
    Z = C // 2
    sib = z * 2 + 1 - k
    nh, chunk = dw.shape[0], dw.shape[1]
    t = masked.shape[0]
    total = rows.shape[1]
    tq = total // R
    nd, dchunk = part.shape[1], part.shape[5]

    weights = []
    for i in range(nh):
        span = pl.ds(i * chunk, chunk)
        weights.append(
            [
                pltpu.make_async_copy(gate_hbm.at[:, span], gw.at[i], w_sem.at[0, i]),
                pltpu.make_async_copy(up_hbm.at[:, span], uw.at[i], w_sem.at[1, i]),
                pltpu.make_async_copy(down_hbm.at[span, :], dw.at[i], w_sem.at[2, i]),
            ]
        )

    barrier = pltpu.get_barrier_semaphore()
    for j in range(1, R):
        pl.semaphore_signal(
            barrier, inc=1, device_id=(lax.rem(r + j, R), c), device_id_type=MESH_ID
        )
    for j in range(1, Z):
        pl.semaphore_signal(
            barrier, inc=1, device_id=(r, lax.rem(z + j, Z) * 2 + k), device_id_type=MESH_ID
        )
    pl.semaphore_signal(barrier, inc=1, device_id=(r, sib), device_id_type=MESH_ID)
    pl.semaphore_wait(barrier, R + Z - 1)

    def block(x, index):
        return rows.at[x, pl.ds(pl.multiple_of(index * t, t), t), :]

    def remote(src, dst, ss, rs, dev):
        return pltpu.make_async_remote_copy(
            src_ref=src,
            dst_ref=dst,
            send_sem=ss,
            recv_sem=rs,
            device_id=dev,
            device_id_type=MESH_ID,
        )

    def gather_far(x, j):
        own = (masked, cot)[x]
        return remote(
            own,
            block(x, c),
            ag_s.at[x, j],
            ag_r.at[x, j],
            (r, lax.rem(z + j, Z) * 2 + k),
        )

    def gather_near(x, j):
        index = lax.rem(z - j + Z, Z) * 2 + k
        src = (masked, cot)[x] if j == 0 else block(x, index)
        return remote(src, block(x, index), fw_s.at[x, j], fw_r.at[x, j], (r, sib))

    for x in range(2):
        for j in range(1, Z):
            gather_far(x, j).start()
        gather_near(x, 0).start()
    for which in range(3):
        for i in range(nh):
            weights[i][which].start()
    rows[0, pl.ds(pl.multiple_of(c * t, t), t), :] = masked[...]
    rows[1, pl.ds(pl.multiple_of(c * t, t), t), :] = cot[...]

    def finish_gather(x):
        for j in range(1, Z):
            gather_far(x, j).wait_recv()
            gather_near(x, j).start()
        for j in range(Z):
            gather_near(x, j).wait_recv()

    def quarter(index):
        return pl.ds(pl.multiple_of(index * tq, tq), tq)

    def gu_copy(i, j):
        p = lax.rem(r + j, R)
        return remote(
            gu_send.at[i, :, quarter(p), :],
            gu_recv.at[i, j - 1],
            gu_ss.at[i, j],
            gu_rs.at[i, j],
            (p, c),
        )

    def gh_copy(i, j):
        p = lax.rem(r + j, R)
        return remote(
            gh_send.at[i, quarter(p), :],
            gh_recv.at[i, j - 1],
            gh_ss.at[i, j],
            gh_rs.at[i, j],
            (p, c),
        )

    def act_copy(a, i, j):
        p = lax.rem(r + j, R)
        return remote(
            act.at[a, i, quarter(r), :],
            act.at[a, i, quarter(r), :],
            act_ss.at[a, i, j],
            act_rs.at[a, i, j],
            (p, c),
        )

    finish_gather(0)
    for i in range(nh):
        weights[i][0].wait()
        weights[i][1].wait()

    def gate_up_step(i, carry):
        gu_send[i, 0] = dot(rows[0], gw[i]).astype(BF16)
        gu_send[i, 1] = dot(rows[0], uw[i]).astype(BF16)
        for j in range(1, R):
            gu_copy(i, j).start()
        return carry

    lax.fori_loop(0, nh, gate_up_step, 0)
    tok_out = pltpu.make_async_copy(rows.at[0], tok_hbm, o_sem.at[0])
    tok_out.start()

    finish_gather(1)
    for i in range(nh):
        weights[i][2].wait()

    def grad_hidden_step(i, carry):
        gh_send[i] = dot_last(rows[1], dw[i]).astype(BF16)
        for j in range(1, R):
            gh_copy(i, j).start()
        return carry

    lax.fori_loop(0, nh, grad_hidden_step, 0)
    cot_out = pltpu.make_async_copy(rows.at[1], cotall_hbm, o_sem.at[1])
    cot_out.start()

    def hidden_step(i, carry):
        for j in range(1, R):
            gu_copy(i, j).wait_recv()
        gate = gu_send[i, 0, quarter(r), :].astype(F32)
        up = gu_send[i, 1, quarter(r), :].astype(F32)
        for j in range(1, R):
            gate = gate + gu_recv[i, j - 1, 0].astype(F32)
            up = up + gu_recv[i, j - 1, 1].astype(F32)
        gate_s[i] = gate
        up_s[i] = up
        act[0, i, quarter(r), :] = (gate * jax.nn.sigmoid(gate) * up).astype(BF16)
        for j in range(1, R):
            act_copy(0, i, j).start()
        return carry

    lax.fori_loop(0, nh, hidden_step, 0)

    def dgate_step(i, carry):
        for j in range(1, R):
            gh_copy(i, j).wait_recv()
        grad = gh_send[i, quarter(r), :].astype(F32)
        for j in range(1, R):
            grad = grad + gh_recv[i, j - 1].astype(F32)
        gate = gate_s[i]
        sig = jax.nn.sigmoid(gate)
        act[1, i, quarter(r), :] = (
            grad * up_s[i] * sig * (1.0 + gate * (1.0 - sig))
        ).astype(BF16)
        act[2, i, quarter(r), :] = (grad * gate * sig).astype(BF16)
        for j in range(1, R):
            act_copy(1, i, j).start()
            act_copy(2, i, j).start()
        return carry

    lax.fori_loop(0, nh, dgate_step, 0)

    def near_sum(x, n):
        return remote(
            part.at[x, n, :, 1 - k],
            sib_recv.at[x, n],
            sib_ss.at[x, n],
            sib_rs.at[x, n],
            (r, sib),
        )

    def far_sum(x, n, j):
        zp = lax.rem(z + j, Z)
        return remote(
            z_send.at[x, n, zp],
            z_recv.at[x, n, j - 1],
            z_ss.at[x, n, j],
            z_rs.at[x, n, j],
            (r, zp * 2 + k),
        )

    def send_part(x, n, value):
        part[x, n] = value.astype(BF16).reshape(Z, 2, t, dchunk)
        near_sum(x, n).start()

    def pass_on(x, n):
        near_sum(x, n).wait_recv()
        z_send[x, n] = (part[x, n, :, k].astype(F32) + sib_recv[x, n].astype(F32)).astype(BF16)
        for j in range(1, Z):
            far_sum(x, n, j).start()

    def collect(x, n):
        for j in range(1, Z):
            far_sum(x, n, j).wait_recv()
        value = z_send[x, n, z].astype(F32)
        for j in range(1, Z):
            value = value + z_recv[x, n, j - 1].astype(F32)
        return value.astype(BF16)

    def act_wait(a):
        def step(i, carry):
            for j in range(1, R):
                act_copy(a, i, j).wait_recv()
            return carry

        lax.fori_loop(0, nh, step, 0)

    act_wait(0)
    hid_out = pltpu.make_async_copy(act.at[0], hid_hbm, o_sem.at[2])
    hid_out.start()
    for n in range(nd):
        cols = slice(n * dchunk, (n + 1) * dchunk)

        def out_step(i, total_value):
            return total_value + dot(act[0, i], dw[i, :, cols])

        send_part(0, n, lax.fori_loop(0, nh, out_step, jnp.zeros((total, dchunk), F32)))
        if n:
            pass_on(0, n - 1)
    pass_on(0, nd - 1)

    act_wait(1)
    dg_out = pltpu.make_async_copy(act.at[1], dg_hbm, o_sem.at[3])
    dg_out.start()
    act_wait(2)
    du_out = pltpu.make_async_copy(act.at[2], du_hbm, o_sem.at[4])
    du_out.start()
    for n in range(nd):
        cols = slice(n * dchunk, (n + 1) * dchunk)

        def mask_step(i, total_value):
            return (
                total_value
                + dot_last(act[1, i], gw[i, cols, :])
                + dot_last(act[2, i], uw[i, cols, :])
            )

        send_part(1, n, lax.fori_loop(0, nh, mask_step, jnp.zeros((total, dchunk), F32)))
        if n:
            pass_on(1, n - 1)
    pass_on(1, nd - 1)

    for n in range(nd):
        out[:, n * dchunk : (n + 1) * dchunk] = collect(0, n)
    for n in range(nd):
        gmask[:, n * dchunk : (n + 1) * dchunk] = collect(1, n)

    for x in range(2):
        for j in range(1, Z):
            gather_far(x, j).wait_send()
        for j in range(Z):
            gather_near(x, j).wait_send()
        for n in range(nd):
            near_sum(x, n).wait_send()
            for j in range(1, Z):
                far_sum(x, n, j).wait_send()

    def drain(i, carry):
        for j in range(1, R):
            gu_copy(i, j).wait_send()
            gh_copy(i, j).wait_send()
            for a in range(3):
                act_copy(a, i, j).wait_send()
        return carry

    lax.fori_loop(0, nh, drain, 0)
    for copy in (tok_out, cot_out, hid_out, dg_out, du_out):
        copy.wait()


def exchange(R, C, masked, cot, gate_weight, up_weight, down_weight):
    t, width = masked.shape
    hidden = gate_weight.shape[1]
    total = t * C
    tq = total // R
    Z = C // 2
    chunk = 256 if hidden % 256 == 0 else hidden
    dchunk = 512 if width % 512 == 0 else width
    nh, nd = hidden // chunk, width // dchunk
    dma = pltpu.SemaphoreType.DMA
    vmem = pl.BlockSpec(memory_space=pltpu.VMEM)
    anywhere = pl.BlockSpec(memory_space=pl.ANY)
    small = jax.ShapeDtypeStruct((t, width), BF16)
    wide = jax.ShapeDtypeStruct((total, width), BF16)
    units = jax.ShapeDtypeStruct((nh, total, chunk), BF16)
    return pl.pallas_call(
        functools.partial(exchange_kernel, R, C),
        out_shape=(small, small, wide, wide, units, units, units),
        in_specs=[vmem, vmem, anywhere, anywhere, anywhere],
        out_specs=(vmem, vmem) + (anywhere,) * 5,
        scratch_shapes=[
            pltpu.VMEM((nh, width, chunk), BF16),
            pltpu.VMEM((nh, width, chunk), BF16),
            pltpu.VMEM((nh, chunk, width), BF16),
            pltpu.VMEM((2, total, width), BF16),
            pltpu.VMEM((nh, 2, total, chunk), BF16),
            pltpu.VMEM((nh, R - 1, 2, tq, chunk), BF16),
            pltpu.VMEM((nh, total, chunk), BF16),
            pltpu.VMEM((nh, R - 1, tq, chunk), BF16),
            pltpu.VMEM((nh, tq, chunk), F32),
            pltpu.VMEM((nh, tq, chunk), F32),
            pltpu.VMEM((3, nh, total, chunk), BF16),
            pltpu.VMEM((2, nd, Z, 2, t, dchunk), BF16),
            pltpu.VMEM((2, nd, Z, t, dchunk), BF16),
            pltpu.VMEM((2, nd, Z, t, dchunk), BF16),
            pltpu.VMEM((2, nd, Z - 1, t, dchunk), BF16),
            dma((3, nh)),
            dma((5,)),
            dma((2, Z)),
            dma((2, Z)),
            dma((2, Z)),
            dma((2, Z)),
            dma((nh, R)),
            dma((nh, R)),
            dma((nh, R)),
            dma((nh, R)),
            dma((3, nh, R)),
            dma((3, nh, R)),
            dma((2, nd)),
            dma((2, nd)),
            dma((2, nd, Z)),
            dma((2, nd, Z)),
        ],
        compiler_params=pltpu.CompilerParams(
            collective_id=0, has_side_effects=True, vmem_limit_bytes=56 * 1024 * 1024
        ),
        cost_estimate=pl.CostEstimate(
            flops=12 * total * width * hidden, bytes_accessed=6 * width * hidden, transcendentals=0
        ),
    )(masked, cot, gate_weight, up_weight, down_weight)


def weight_grad_kernel(tok, cot, hid, dg, du, grad_gate, grad_up, grad_down, tok_t):
    @pl.when(pl.program_id(0) == 0)
    def _():
        tok_t[...] = tok[...].T

    grad_gate[...] = dot(tok_t[...], dg[0]).astype(BF16)
    grad_up[...] = dot(tok_t[...], du[0]).astype(BF16)
    grad_down[...] = lax.dot_general(
        hid[0], cot[...], FIRST, preferred_element_type=F32
    ).astype(BF16)


def weight_grads(tok, cot, hid, dg, du):
    total, width = tok.shape
    nh, _, chunk = hid.shape
    hidden = nh * chunk
    whole = pl.BlockSpec((total, width), lambda i: (0, 0))
    unit = pl.BlockSpec((1, total, chunk), lambda i: (i, 0, 0))
    across = jax.ShapeDtypeStruct((width, hidden), BF16)
    return pl.pallas_call(
        weight_grad_kernel,
        grid=(nh,),
        out_shape=(across, across, jax.ShapeDtypeStruct((hidden, width), BF16)),
        in_specs=[whole, whole, unit, unit, unit],
        out_specs=(
            pl.BlockSpec((width, chunk), lambda i: (0, i)),
            pl.BlockSpec((width, chunk), lambda i: (0, i)),
            pl.BlockSpec((chunk, width), lambda i: (i, 0)),
        ),
        scratch_shapes=[pltpu.VMEM((width, total), BF16)],
        compiler_params=pltpu.CompilerParams(vmem_limit_bytes=48 * 1024 * 1024),
        cost_estimate=pl.CostEstimate(
            flops=6 * total * width * hidden, bytes_accessed=6 * width * hidden, transcendentals=0
        ),
    )(tok, cot, hid, dg, du)


def shards(
    R,
    C,
    frames,
    cotangent,
    gate_weight,
    up_weight,
    down_weight,
    utt_ids,
    valid_len,
    time_start,
    time_width,
    freq_start,
    freq_width,
):
    tok_rows, feat_cols = frames.shape
    first_tok = lax.axis_index("col") * tok_rows
    first_feat = lax.axis_index("row") * feat_cols
    tok_index = first_tok + jnp.arange(tok_rows, dtype=jnp.int32)
    feat_index = first_feat + jnp.arange(feat_cols, dtype=jnp.int32)
    local_ids = lax.dynamic_slice_in_dim(utt_ids, first_tok, tok_rows)
    keep_mask, valid_rows = span_masks(
        utt_ids,
        local_ids,
        tok_index,
        feat_index,
        valid_len,
        time_start,
        time_width,
        freq_start,
        freq_width,
    )
    masked = jnp.where(keep_mask, frames, jnp.zeros_like(frames))
    cot_valid = jnp.where(valid_rows[:, None], cotangent, jnp.zeros_like(cotangent))
    output, grad_masked, tok, cot, hid, dg, du = exchange(
        R, C, masked, cot_valid, gate_weight, up_weight, down_weight
    )
    grad_gate, grad_up, grad_down = weight_grads(tok, cot, hid, dg, du)
    grad_frames = jnp.where(keep_mask, grad_masked, jnp.zeros_like(grad_masked))
    return (output, grad_frames, grad_gate, grad_up, grad_down)


def solution(mesh):
    placed = (
        P("col", "row"),
        P("col", "row"),
        P("row", "col"),
        P("row", "col"),
        P("col", "row"),
        P(),
        P(),
        P(),
        P(),
        P(),
        P(),
    )
    return jax.shard_map(
        functools.partial(shards, mesh.shape["row"], mesh.shape["col"]),
        mesh=mesh,
        in_specs=placed,
        out_specs=(
            P("col", "row"),
            P("col", "row"),
            P("row", "col"),
            P("row", "col"),
            P("col", "row"),
        ),
        check_vma=False,
    )
```

```python
import functools
import jax
import jax.numpy as jnp
from jax import lax
from jax.experimental import pallas as pl
from jax.experimental.pallas import tpu as pltpu
from jax.sharding import PartitionSpec as P


def span_masks(
    utt_ids,
    local_ids,
    tok_index,
    feat_index,
    valid_len,
    time_start,
    time_width,
    freq_start,
    freq_width,
):
    utt_index = jnp.arange(valid_len.shape[0], dtype=jnp.int32)
    starts = jnp.sum((utt_ids[None, :] < utt_index[:, None]).astype(jnp.int32), axis=1)
    member = (local_ids[:, None] == utt_index[None, :]).astype(jnp.int32)

    def lookup(table):
        return jnp.sum(member * table[None, :], axis=1)

    position = tok_index - lookup(starts)
    valid_rows = position < lookup(valid_len)
    time_low = lookup(time_start)
    in_time = (position >= time_low) & (position < time_low + lookup(time_width))
    freq_low = lookup(freq_start)[:, None]
    freq_high = freq_low + lookup(freq_width)[:, None]
    in_freq = (feat_index[None, :] >= freq_low) & (feat_index[None, :] < freq_high)
    keep_mask = (valid_rows & jnp.logical_not(in_time))[:, None] & jnp.logical_not(in_freq)
    return (keep_mask, valid_rows)


MESH_ID = pl.DeviceIdType.MESH
LAST = (((1,), (1,)), ((), ()))
FIRST = (((0,), (0,)), ((), ()))
F32 = jnp.float32
BF16 = jnp.bfloat16


def dot(a, b):
    return jnp.dot(a, b, preferred_element_type=F32)


def dot_last(a, b):
    return lax.dot_general(a, b, LAST, preferred_element_type=F32)


def exchange_kernel(
    R,
    C,
    masked,
    cot,
    gate_hbm,
    up_hbm,
    down_hbm,
    out,
    gmask,
    tok_hbm,
    cotall_hbm,
    hid_hbm,
    dg_hbm,
    du_hbm,
    gw,
    uw,
    dw,
    rows,
    gu_send,
    gu_recv,
    gu_fwd,
    gh_send,
    gh_recv,
    gh_fwd,
    gate_s,
    up_s,
    act,
    part,
    sib_recv,
    z_send,
    z_recv,
    w_sem,
    o_sem,
    ag_s,
    ag_r,
    fw_s,
    fw_r,
    gu_ss,
    gu_rs,
    gh_ss,
    gh_rs,
    act_ss,
    act_rs,
    sib_ss,
    sib_rs,
    z_ss,
    z_rs,
):
    r = lax.axis_index("row")
    c = lax.axis_index("col")
    z = c // 2
    k = c % 2
    Z = C // 2
    sib = z * 2 + 1 - k
    nh, chunk = dw.shape[0], dw.shape[1]
    t = masked.shape[0]
    total = rows.shape[1]
    tq = total // R
    nd, dchunk = part.shape[1], part.shape[5]

    weights = []
    for i in range(nh):
        span = pl.ds(i * chunk, chunk)
        weights.append(
            [
                pltpu.make_async_copy(gate_hbm.at[:, span], gw.at[i], w_sem.at[0, i]),
                pltpu.make_async_copy(up_hbm.at[:, span], uw.at[i], w_sem.at[1, i]),
                pltpu.make_async_copy(down_hbm.at[span, :], dw.at[i], w_sem.at[2, i]),
            ]
        )

    barrier = pltpu.get_barrier_semaphore()
    for j in range(1, R):
        pl.semaphore_signal(
            barrier, inc=1, device_id=(lax.rem(r + j, R), c), device_id_type=MESH_ID
        )
    for j in range(1, Z):
        pl.semaphore_signal(
            barrier, inc=1, device_id=(r, lax.rem(z + j, Z) * 2 + k), device_id_type=MESH_ID
        )
    pl.semaphore_signal(barrier, inc=1, device_id=(r, sib), device_id_type=MESH_ID)
    pl.semaphore_wait(barrier, R + Z - 1)

    def block(x, index):
        return rows.at[x, pl.ds(pl.multiple_of(index * t, t), t), :]

    def remote(src, dst, ss, rs, dev):
        return pltpu.make_async_remote_copy(
            src_ref=src,
            dst_ref=dst,
            send_sem=ss,
            recv_sem=rs,
            device_id=dev,
            device_id_type=MESH_ID,
        )

    def gather_far(x, j):
        own = (masked, cot)[x]
        return remote(
            own,
            block(x, c),
            ag_s.at[x, j],
            ag_r.at[x, j],
            (r, lax.rem(z + j, Z) * 2 + k),
        )

    def gather_near(x, j):
        index = lax.rem(z - j + Z, Z) * 2 + k
        src = (masked, cot)[x] if j == 0 else block(x, index)
        return remote(src, block(x, index), fw_s.at[x, j], fw_r.at[x, j], (r, sib))

    def start_gather(x):
        for j in range(1, Z):
            gather_far(x, j).start()
        gather_near(x, 0).start()

    start_gather(0)
    for which in range(3):
        for i in range(nh):
            weights[i][which].start()
    rows[0, pl.ds(pl.multiple_of(c * t, t), t), :] = masked[...]
    rows[1, pl.ds(pl.multiple_of(c * t, t), t), :] = cot[...]

    def finish_gather(x):
        for j in range(1, Z):
            gather_far(x, j).wait_recv()
            gather_near(x, j).start()
        for j in range(Z):
            gather_near(x, j).wait_recv()

    def quarter(index):
        return pl.ds(pl.multiple_of(index * tq, tq), tq)

    square = R == 4
    D = 2 if square else 1
    h = tq // D
    side = (r + 1 - 2 * (r % 2), r + 2 - 4 * (r // 2))
    corner = 3 - r

    def half(index, d):
        return pl.ds(pl.multiple_of(index * tq + d * h, h), h)

    def share(refs, i, index, d):
        return refs[0].at[(i,) + (slice(None),) * (len(refs[0].shape) - 3) + (half(index, d),)]

    def row_copy(refs, i, d, s):
        send, recv, fwd, ss, rs = refs
        if not square:
            p = lax.rem(r + s + 1, R)
            src = share(refs, i, p, 0)
        elif s == 2:
            p = side[1 - d]
            src = fwd.at[i, d]
        else:
            p = side[d]
            src = share(refs, i, (side[d], corner)[s], d)
        return remote(src, recv.at[i, d, s], ss.at[i, d, s], rs.at[i, d, s], (p, c))

    first_slots = (1, 0) if square else range(R - 1)
    last_slots = (0, 2) if square else range(R - 1)

    def row_start(refs, i):
        for s in first_slots:
            for d in range(D):
                row_copy(refs, i, d, s).start()

    def row_pass(refs, i):
        if square:
            for d in range(D):
                row_copy(refs, i, d, 1).wait_recv()
                mine = share(refs, i, side[1 - d], d)[...].astype(F32)
                refs[2][i, d] = (mine + refs[1][i, d, 1].astype(F32)).astype(BF16)
                row_copy(refs, i, d, 2).start()

    def row_total(refs, i, d):
        for s in last_slots:
            row_copy(refs, i, d, s).wait_recv()
        value = share(refs, i, r, d)[...].astype(F32)
        for s in last_slots:
            value = value + refs[1][i, d, s].astype(F32)
        return value

    gu = (gu_send, gu_recv, gu_fwd, gu_ss, gu_rs)
    gh = (gh_send, gh_recv, gh_fwd, gh_ss, gh_rs)

    def act_copy(a, i, s):
        if not square:
            p, rows_of = lax.rem(r + s + 1, R), quarter(r)
        elif s < 2:
            p, rows_of = side[s], quarter(r)
        else:
            p, rows_of = side[3 - s], half(side[s - 2], s - 2)
        return remote(
            act.at[a, i, rows_of, :],
            act.at[a, i, rows_of, :],
            act_ss.at[a, i, s],
            act_rs.at[a, i, s],
            (p, c),
        )

    act_slots = range(4) if square else range(R - 1)

    def act_start(a, i):
        for s in range(2) if square else act_slots:
            act_copy(a, i, s).start()

    def act_pass(a, i):
        if square:
            for s in range(2):
                act_copy(a, i, s).wait_recv()
                act_copy(a, i, s + 2).start()

    def act_wait(a):
        def step(i, carry):
            for s in (2, 3) if square else act_slots:
                act_copy(a, i, s).wait_recv()
            return carry

        lax.fori_loop(0, nh, step, 0)

    lag = min(2, nh)

    finish_gather(0)
    start_gather(1)
    for i in range(nh):
        weights[i][0].wait()
        weights[i][1].wait()

    def gate_up_step(i, carry):
        gu_send[i, 0] = dot(rows[0], gw[i]).astype(BF16)
        gu_send[i, 1] = dot(rows[0], uw[i]).astype(BF16)
        row_start(gu, i)

        @pl.when(i >= lag)
        def _():
            row_pass(gu, i - lag)

        return carry

    lax.fori_loop(0, nh, gate_up_step, 0)
    tok_out = pltpu.make_async_copy(rows.at[0], tok_hbm, o_sem.at[0])
    tok_out.start()

    finish_gather(1)
    for i in range(nh):
        weights[i][2].wait()

    def grad_hidden_step(i, carry):
        gh_send[i] = dot_last(rows[1], dw[i]).astype(BF16)
        row_start(gh, i)

        @pl.when(i < lag)
        def _():
            row_pass(gu, nh - lag + i)

        @pl.when(i >= lag)
        def _():
            row_pass(gh, i - lag)

        for d in range(D):
            both = row_total(gu, i, d)
            gate, up = both[0], both[1]
            gate_s[i, d] = gate
            up_s[i, d] = up
            act[0, i, half(r, d), :] = (gate * jax.nn.sigmoid(gate) * up).astype(BF16)
        act_start(0, i)
        return carry

    lax.fori_loop(0, nh, grad_hidden_step, 0)
    cot_out = pltpu.make_async_copy(rows.at[1], cotall_hbm, o_sem.at[1])
    cot_out.start()

    def dgate_step(i, carry):
        @pl.when(i < lag)
        def _():
            row_pass(gh, nh - lag + i)

        act_pass(0, i)
        for d in range(D):
            grad = row_total(gh, i, d)
            gate = gate_s[i, d]
            sig = jax.nn.sigmoid(gate)
            act[1, i, half(r, d), :] = (
                grad * up_s[i, d] * sig * (1.0 + gate * (1.0 - sig))
            ).astype(BF16)
            act[2, i, half(r, d), :] = (grad * gate * sig).astype(BF16)
        act_start(1, i)
        act_start(2, i)
        return carry

    lax.fori_loop(0, nh, dgate_step, 0)

    def grads_pass(low, high):
        def step(i, carry):
            act_pass(1, i)
            act_pass(2, i)
            return carry

        lax.fori_loop(low, high, step, 0)

    def near_sum(x, n):
        return remote(
            part.at[x, n, :, 1 - k],
            sib_recv.at[x, n],
            sib_ss.at[x, n],
            sib_rs.at[x, n],
            (r, sib),
        )

    def far_sum(x, n, j):
        zp = lax.rem(z + j, Z)
        return remote(
            z_send.at[x, n, zp],
            z_recv.at[x, n, j - 1],
            z_ss.at[x, n, j],
            z_rs.at[x, n, j],
            (r, zp * 2 + k),
        )

    def send_part(x, n, value):
        part[x, n] = value.astype(BF16).reshape(Z, 2, t, dchunk)
        near_sum(x, n).start()

    def pass_on(x, n):
        near_sum(x, n).wait_recv()
        z_send[x, n] = (part[x, n, :, k].astype(F32) + sib_recv[x, n].astype(F32)).astype(BF16)
        for j in range(1, Z):
            far_sum(x, n, j).start()

    def collect(x, n):
        for j in range(1, Z):
            far_sum(x, n, j).wait_recv()
        value = z_send[x, n, z].astype(F32)
        for j in range(1, Z):
            value = value + z_recv[x, n, j - 1].astype(F32)
        return value.astype(BF16)

    act_wait(0)
    hid_out = pltpu.make_async_copy(act.at[0], hid_hbm, o_sem.at[2])
    hid_out.start()
    for n in range(nd):
        cols = slice(n * dchunk, (n + 1) * dchunk)

        def out_step(i, total_value):
            return total_value + dot(act[0, i], dw[i, :, cols])

        send_part(0, n, lax.fori_loop(0, nh, out_step, jnp.zeros((total, dchunk), F32)))
        grads_pass(n * nh // nd, (n + 1) * nh // nd)
        if n:
            pass_on(0, n - 1)
    pass_on(0, nd - 1)

    act_wait(1)
    dg_out = pltpu.make_async_copy(act.at[1], dg_hbm, o_sem.at[3])
    dg_out.start()
    act_wait(2)
    du_out = pltpu.make_async_copy(act.at[2], du_hbm, o_sem.at[4])
    du_out.start()
    for n in range(nd):
        cols = slice(n * dchunk, (n + 1) * dchunk)

        def mask_step(i, total_value):
            return (
                total_value
                + dot_last(act[1, i], gw[i, cols, :])
                + dot_last(act[2, i], uw[i, cols, :])
            )

        send_part(1, n, lax.fori_loop(0, nh, mask_step, jnp.zeros((total, dchunk), F32)))
        if n:
            pass_on(1, n - 1)
    pass_on(1, nd - 1)

    for n in range(nd):
        out[:, n * dchunk : (n + 1) * dchunk] = collect(0, n)
    for n in range(nd):
        gmask[:, n * dchunk : (n + 1) * dchunk] = collect(1, n)

    for x in range(2):
        for j in range(1, Z):
            gather_far(x, j).wait_send()
        for j in range(Z):
            gather_near(x, j).wait_send()
        for n in range(nd):
            near_sum(x, n).wait_send()
            for j in range(1, Z):
                far_sum(x, n, j).wait_send()

    def drain(i, carry):
        for d in range(D):
            for s in range(R - 1):
                row_copy(gu, i, d, s).wait_send()
                row_copy(gh, i, d, s).wait_send()
        for a in range(3):
            for s in act_slots:
                act_copy(a, i, s).wait_send()
        return carry

    lax.fori_loop(0, nh, drain, 0)
    for copy in (tok_out, cot_out, hid_out, dg_out, du_out):
        copy.wait()


def exchange(R, C, masked, cot, gate_weight, up_weight, down_weight):
    t, width = masked.shape
    hidden = gate_weight.shape[1]
    total = t * C
    tq = total // R
    D = 2 if R == 4 else 1
    h = tq // D
    Z = C // 2
    chunk = 256 if hidden % 256 == 0 else hidden
    dchunk = 512 if width % 512 == 0 else width
    nh, nd = hidden // chunk, width // dchunk
    dma = pltpu.SemaphoreType.DMA
    vmem = pl.BlockSpec(memory_space=pltpu.VMEM)
    anywhere = pl.BlockSpec(memory_space=pl.ANY)
    small = jax.ShapeDtypeStruct((t, width), BF16)
    wide = jax.ShapeDtypeStruct((total, width), BF16)
    units = jax.ShapeDtypeStruct((nh, total, chunk), BF16)
    return pl.pallas_call(
        functools.partial(exchange_kernel, R, C),
        out_shape=(small, small, wide, wide, units, units, units),
        in_specs=[vmem, vmem, anywhere, anywhere, anywhere],
        out_specs=(vmem, vmem) + (anywhere,) * 5,
        scratch_shapes=[
            pltpu.VMEM((nh, width, chunk), BF16),
            pltpu.VMEM((nh, width, chunk), BF16),
            pltpu.VMEM((nh, chunk, width), BF16),
            pltpu.VMEM((2, total, width), BF16),
            pltpu.VMEM((nh, 2, total, chunk), BF16),
            pltpu.VMEM((nh, D, R - 1, 2, h, chunk), BF16),
            pltpu.VMEM((nh, D, 2, h, chunk), BF16),
            pltpu.VMEM((nh, total, chunk), BF16),
            pltpu.VMEM((nh, D, R - 1, h, chunk), BF16),
            pltpu.VMEM((nh, D, h, chunk), BF16),
            pltpu.VMEM((nh, D, h, chunk), F32),
            pltpu.VMEM((nh, D, h, chunk), F32),
            pltpu.VMEM((3, nh, total, chunk), BF16),
            pltpu.VMEM((2, nd, Z, 2, t, dchunk), BF16),
            pltpu.VMEM((2, nd, Z, t, dchunk), BF16),
            pltpu.VMEM((2, nd, Z, t, dchunk), BF16),
            pltpu.VMEM((2, nd, Z - 1, t, dchunk), BF16),
            dma((3, nh)),
            dma((5,)),
            dma((2, Z)),
            dma((2, Z)),
            dma((2, Z)),
            dma((2, Z)),
            dma((nh, D, R - 1)),
            dma((nh, D, R - 1)),
            dma((nh, D, R - 1)),
            dma((nh, D, R - 1)),
            dma((3, nh, max(R - 1, 4))),
            dma((3, nh, max(R - 1, 4))),
            dma((2, nd)),
            dma((2, nd)),
            dma((2, nd, Z)),
            dma((2, nd, Z)),
        ],
        compiler_params=pltpu.CompilerParams(
            collective_id=0, has_side_effects=True, vmem_limit_bytes=56 * 1024 * 1024
        ),
        cost_estimate=pl.CostEstimate(
            flops=12 * total * width * hidden, bytes_accessed=6 * width * hidden, transcendentals=0
        ),
    )(masked, cot, gate_weight, up_weight, down_weight)


def weight_grad_kernel(tok, cot, hid, dg, du, grad_gate, grad_up, grad_down, tok_t):
    @pl.when(pl.program_id(0) == 0)
    def _():
        tok_t[...] = tok[...].T

    grad_gate[...] = dot(tok_t[...], dg[0]).astype(BF16)
    grad_up[...] = dot(tok_t[...], du[0]).astype(BF16)
    grad_down[...] = lax.dot_general(
        hid[0], cot[...], FIRST, preferred_element_type=F32
    ).astype(BF16)


def weight_grads(tok, cot, hid, dg, du):
    total, width = tok.shape
    nh, _, chunk = hid.shape
    hidden = nh * chunk
    whole = pl.BlockSpec((total, width), lambda i: (0, 0))
    unit = pl.BlockSpec((1, total, chunk), lambda i: (i, 0, 0))
    across = jax.ShapeDtypeStruct((width, hidden), BF16)
    return pl.pallas_call(
        weight_grad_kernel,
        grid=(nh,),
        out_shape=(across, across, jax.ShapeDtypeStruct((hidden, width), BF16)),
        in_specs=[whole, whole, unit, unit, unit],
        out_specs=(
            pl.BlockSpec((width, chunk), lambda i: (0, i)),
            pl.BlockSpec((width, chunk), lambda i: (0, i)),
            pl.BlockSpec((chunk, width), lambda i: (i, 0)),
        ),
        scratch_shapes=[pltpu.VMEM((width, total), BF16)],
        compiler_params=pltpu.CompilerParams(vmem_limit_bytes=62 * 1024 * 1024),
        cost_estimate=pl.CostEstimate(
            flops=6 * total * width * hidden, bytes_accessed=6 * width * hidden, transcendentals=0
        ),
    )(tok, cot, hid, dg, du)


def shards(
    R,
    C,
    frames,
    cotangent,
    gate_weight,
    up_weight,
    down_weight,
    utt_ids,
    valid_len,
    time_start,
    time_width,
    freq_start,
    freq_width,
):
    tok_rows, feat_cols = frames.shape
    first_tok = lax.axis_index("col") * tok_rows
    first_feat = lax.axis_index("row") * feat_cols
    tok_index = first_tok + jnp.arange(tok_rows, dtype=jnp.int32)
    feat_index = first_feat + jnp.arange(feat_cols, dtype=jnp.int32)
    local_ids = lax.dynamic_slice_in_dim(utt_ids, first_tok, tok_rows)
    keep_mask, valid_rows = span_masks(
        utt_ids,
        local_ids,
        tok_index,
        feat_index,
        valid_len,
        time_start,
        time_width,
        freq_start,
        freq_width,
    )
    masked = jnp.where(keep_mask, frames, jnp.zeros_like(frames))
    cot_valid = jnp.where(valid_rows[:, None], cotangent, jnp.zeros_like(cotangent))
    output, grad_masked, tok, cot, hid, dg, du = exchange(
        R, C, masked, cot_valid, gate_weight, up_weight, down_weight
    )
    grad_gate, grad_up, grad_down = weight_grads(tok, cot, hid, dg, du)
    grad_frames = jnp.where(keep_mask, grad_masked, jnp.zeros_like(grad_masked))
    return (output, grad_frames, grad_gate, grad_up, grad_down)


def solution(mesh):
    placed = (
        P("col", "row"),
        P("col", "row"),
        P("row", "col"),
        P("row", "col"),
        P("col", "row"),
        P(),
        P(),
        P(),
        P(),
        P(),
        P(),
    )
    return jax.shard_map(
        functools.partial(shards, mesh.shape["row"], mesh.shape["col"]),
        mesh=mesh,
        in_specs=placed,
        out_specs=(
            P("col", "row"),
            P("col", "row"),
            P("row", "col"),
            P("row", "col"),
            P("col", "row"),
        ),
        check_vma=False,
    )
```
